256 devices in a mesh: side: 2 (over z_hi), brick: 128 (over z_lo, x, y, core).
Axes of the slice: x: 4, y: 4, z: 8 (z_hi: 2, z_lo: 4; z = z_hi * 4 + z_lo), core: 2. Of those that a mesh axis runs over, the one named last changes fastest.
Arguments:
- fields: float32 [10, 128, 256, 256], P('side', 'brick'), may hold values from -6 to 6
- source_field: float32 [128, 256, 256], P('brick'), may hold values from -6 to 6
- params_a: float32 [8], replicated, may hold values from 0 to 1
- params_b: float32 [8], replicated, may hold values from 0 to 1
- running_means: float32 [10, 128, 256, 256], P(None, None, ('side', 'brick')), may hold values from -6 to 6
- running_squares: float32 [10, 128, 256, 256], P(None, None, ('side', 'brick')), as said below
- running_cross: float32 [16, 128, 256, 256], P(None, None, ('side', 'brick')), as said below
Outputs:
- new_means: float32 [10, 128, 256, 256], P(None, None, ('side', 'brick'))
- new_squares: float32 [10, 128, 256, 256], P(None, None, ('side', 'brick'))
- new_cross: float32 [16, 128, 256, 256], P(None, None, ('side', 'brick'))
- sobol_maps: float32 [16, 128, 256, 256], P(None, None, ('side', 'brick'))
The draws below stay inside these ranges and needn't reach their ends.
Inputs may be any that keep to these rules, and one draw needn't show every extreme that they name: `running_squares`: Positive. `running_cross`: each entry lies within 0.8 sqrt of the product of the two members' running_squares in magnitude.
All inputs are finite; a program needn't handle non-finite values.
Results may differ from the reference program's by a relative error of at most 0.00002.
Values sent between devices are 32-bit elements; how exact they have to be, the bound alone decides.
No kernel may reach another device: no remote copies, remote signals or barrier semaphores. Data moves between devices by JAX's collectives and lax.ppermute only.
A program may use at most 64 MiB of HBM per device.

```python
import jax
import jax.numpy as jnp

PARAMS = 8
MEMBERS = 10
PRIOR = 3
NZ = 256
NX = 128
NY = 256


def moment_sizes(key, lowest, highest):
    unit = jax.random.uniform(key, (MEMBERS, NX, NY, NZ), jnp.float32)
    return PRIOR * jnp.exp(jnp.log(lowest) + unit * jnp.log(highest / lowest))


def draw_running_squares(key, part):
    lowest = 0.5
    highest = 3.0
    shared = moment_sizes(key, lowest, highest)
    return shared


def draw_running_cross(key, part):
    lowest = 0.5
    highest = 3.0
    shared = moment_sizes(key, lowest, highest)
    key = jax.random.fold_in(key, 7)
    ratio = jax.random.uniform(key, (2 * PARAMS, NX, NY, NZ), jnp.float32, -0.8, 0.8)
    first_part = ratio[:PARAMS] * jnp.sqrt(shared[1:2] * shared[2:])
    total_part = ratio[PARAMS:] * jnp.sqrt(shared[0:1] * shared[2:])
    return jnp.concatenate([first_part, total_part], axis=0)


def block_levels(rng, dims, pieces, least, top_value):
    def one(dim, shards_of):
        draws = jax.random.uniform(jax.random.fold_in(jax.random.fold_in(rng, 6), dim), (shards_of,), jnp.float32, least / len(pieces), top_value / len(pieces))
        return jnp.repeat(jnp.exp(draws), dims[dim] // shards_of).reshape((-1,) + (1,) * (len(dims) - dim - 1))

    factor_of = one(*pieces[0])
    for cut in pieces[1:]:
        factor_of = factor_of * one(*cut)
    return factor_of


def normal_values(own_key, extent, scale, limit, split=(), held_as=jnp.bfloat16):
    loudness = block_levels(own_key, extent, split, -0.22, 0.18) if split else 1.0
    drawn = jax.random.normal(own_key, extent, jnp.float32) * scale * loudness
    return jnp.minimum(jnp.maximum(drawn, -limit), limit).astype(held_as)


def setup_inputs(seed: int = 0) -> dict:
    key_of = jax.random.split(jax.random.key(seed), 8)
    return {
        "fields": normal_values(key_of[0], (MEMBERS, NX, NY, NZ), 1.0, 6.0, ((0, 2), (1, 128)), jnp.float32),
        "source_field": normal_values(key_of[1], (NX, NY, NZ), 1.0, 6.0, ((0, 128),), jnp.float32),
        "params_a": jnp.clip(jax.random.uniform(key_of[2], (PARAMS,), jnp.float32, 0.0, 1.0), 0.0, 1.0),
        "params_b": jnp.clip(jax.random.uniform(key_of[3], (PARAMS,), jnp.float32, 0.0, 1.0), 0.0, 1.0),
        "running_means": normal_values(key_of[4], (MEMBERS, NX, NY, NZ), 1.0, 6.0, ((2, 256),), jnp.float32),
        "running_squares": draw_running_squares(jax.random.fold_in(key_of[7], 71), 0),
        "running_cross": draw_running_cross(jax.random.fold_in(key_of[7], 71), 0),
    }


lower_bounds = (0.02, 0.02, 0.02, 0.01, 0.0, 0.0, 0.5, 0.0)
upper_bounds = (0.12, 0.12, 0.12, 0.06, 0.2, 1.0, 1.5, 0.1)

def member_theta(members, params_a, params_b):
    column = jnp.arange(params_a.shape[0], dtype=jnp.int32)
    from_b = (members[:, None] == 1) | (members[:, None] == column[None, :] + 2)
    unit = jnp.where(from_b, params_b[None, :], params_a[None, :])
    lower = jnp.asarray(lower_bounds, dtype=params_a.dtype)
    upper = jnp.asarray(upper_bounds, dtype=params_a.dtype)
    return lower[None, :] + (upper - lower)[None, :] * unit

def column_of(physical, index):
    return physical[:, index][:, None, None, None]

def stencil_update(current, physical, source_field, upwind_a, downwind_a, upwind_b, downwind_b, upwind_c, downwind_c):
    drift_first = column_of(physical, 0)
    drift_second = column_of(physical, 1)
    drift_third = column_of(physical, 2)
    diffusion = column_of(physical, 3)
    decay_rate = column_of(physical, 4)
    amplitude = column_of(physical, 5)
    anisotropy = column_of(physical, 6)
    reaction = column_of(physical, 7)
    laplace = upwind_a + downwind_a + upwind_b + downwind_b + anisotropy * (upwind_c + downwind_c) - (4.0 + 2.0 * anisotropy) * current
    change = -drift_first * (current - upwind_a) - drift_second * (current - upwind_b) - drift_third * (current - upwind_c)
    change = change + diffusion * laplace - decay_rate * current - reaction * current * jnp.abs(current)
    change = change + amplitude * source_field[None]
    return current + change

def advance(current, physical, source_field):
    padded = jnp.pad(current, ((0, 0), (1, 1), (1, 1), (1, 1)))
    return stencil_update(current, physical, source_field, padded[:, :-2, 1:-1, 1:-1], padded[:, 2:, 1:-1, 1:-1], padded[:, 1:-1, :-2, 1:-1], padded[:, 1:-1, 2:, 1:-1], padded[:, 1:-1, 1:-1, :-2], padded[:, 1:-1, 1:-1, 2:])

def accumulate(outputs, running_means, running_squares, running_cross):
    total_count = float(PRIOR + 1)
    deviation = outputs - running_means
    new_means = running_means + deviation / total_count
    after = outputs - new_means
    new_squares = running_squares + deviation * after
    count_params = running_cross.shape[0] // 2
    first_cross = running_cross[:count_params] + deviation[1:2] * after[2:]
    total_cross = running_cross[count_params:] + deviation[0:1] * after[2:]
    new_cross = jnp.concatenate([first_cross, total_cross], axis=0)
    first_index = first_cross / jnp.sqrt(new_squares[1:2] * new_squares[2:])
    total_index = 1.0 - total_cross / jnp.sqrt(new_squares[0:1] * new_squares[2:])
    sobol_maps = jnp.concatenate([first_index, total_index], axis=0)
    return (new_means, new_squares, new_cross, sobol_maps)

def reference(fields, source_field, params_a, params_b, running_means, running_squares, running_cross):
    members = jnp.arange(fields.shape[0], dtype=jnp.int32)
    physical = member_theta(members, params_a, params_b)
    current = advance(fields, physical, source_field)
    current = advance(current, physical, source_field)
    new_means, new_squares, new_cross, sobol_maps = accumulate(current, running_means, running_squares, running_cross)
    return (new_means, new_squares, new_cross, sobol_maps)
```

```python
import functools

import jax
import jax.numpy as jnp
import numpy as np
from jax import lax
from jax.experimental import pallas as pl
from jax.experimental.pallas import tpu as pltpu
from jax.sharding import PartitionSpec as P

PRIOR = 3
LOWER = np.asarray((0.02, 0.02, 0.02, 0.01, 0.0, 0.0, 0.5, 0.0), np.float32)
UPPER = np.asarray((0.12, 0.12, 0.12, 0.06, 0.2, 1.0, 1.5, 0.1), np.float32)
WIDTH = UPPER - LOWER
ROWS = 64
CHUNKS = (3, 2)


def physical_of(member, a_ref, b_ref):
    values = []
    for k in range(8):
        from_b = (member == 1) | (member == k + 2)
        unit = jnp.where(from_b, b_ref[k], a_ref[k])
        values.append(float(LOWER[k]) + float(WIDTH[k]) * unit)
    return values


def stencil_kernel(firsts, counts, strided, place_ref, a_ref, b_ref, source_ref, *refs):
    parts, outs = refs[: 3 * len(counts)], refs[3 * len(counts) :]
    side, core = place_ref[0], place_ref[1]
    ny, nz = source_ref.shape
    column = lax.broadcasted_iota(jnp.int32, (ROWS, nz), 1)
    zero = jnp.zeros((8, nz), jnp.float32)
    pieces = nz // 128
    pitch = sum(counts) * pieces
    done = 0
    for i, (first, count) in enumerate(zip(firsts, counts)):
        c_ref, near_ref, far_ref = parts[3 * i : 3 * i + 3]
        out_ref = outs[0] if strided else outs[i]

        def one_member(m, carry, c_ref=c_ref, near_ref=near_ref, far_ref=far_ref, out_ref=out_ref, first=first, done=done):
            drift_1, drift_2, drift_3, diffusion, decay, amplitude, anisotropy, reaction = physical_of(
                side * 5 + first + m, a_ref, b_ref
            )
            along = diffusion * anisotropy
            before = drift_1 + diffusion
            near_w = jnp.where(core == 0, diffusion, before)
            far_w = jnp.where(core == 0, before, diffusion)
            own_w = 1.0 - drift_1 - drift_2 - drift_3 - decay - diffusion * (4.0 + 2.0 * anisotropy)
            for r in range(0, ny, ROWS):
                c = c_ref[m, r : r + ROWS, :]
                above = c_ref[m, r - 8 : r, :] if r > 0 else zero
                below = c_ref[m, r + ROWS : r + ROWS + 8, :] if r + ROWS < ny else zero
                wide = jnp.concatenate([above, c, below], axis=0)
                y_before = pltpu.roll(wide, 1, 0)[8 : 8 + ROWS]
                y_after = pltpu.roll(wide, ROWS + 15, 0)[8 : 8 + ROWS]
                z_before = jnp.where(column == 0, 0.0, pltpu.roll(c, 1, 1))
                z_after = jnp.where(column == nz - 1, 0.0, pltpu.roll(c, nz - 1, 1))
                new = (
                    c * (own_w - reaction * jnp.abs(c))
                    + near_w * near_ref[m, r : r + ROWS, :]
                    + far_w * far_ref[m, r : r + ROWS, :]
                    + (drift_2 + diffusion) * y_before
                    + diffusion * y_after
                    + (drift_3 + along) * z_before
                    + along * z_after
                    + amplitude * source_ref[r : r + ROWS, :]
                )
                if strided:
                    for h in range(pieces):
                        start = r * pitch + (done + m) * pieces + h
                        out_ref[pl.ds(start, ROWS, stride=pitch), :] = new[:, h * 128 : (h + 1) * 128]
                else:
                    out_ref[m, r : r + ROWS, :] = new
            return carry

        lax.fori_loop(0, count, one_member, 0)
        done += count


def advance(place, params_a, params_b, source, parts, firsts, strided):
    counts = [own.shape[0] for own, _, _ in parts]
    ny, nz = source.shape
    whole = pl.BlockSpec(memory_space=pltpu.VMEM)
    scalars = pl.BlockSpec(memory_space=pltpu.SMEM)
    cells = sum(counts) * ny * nz
    if strided:
        out_shape = [jax.ShapeDtypeStruct((cells // 128, 128), jnp.float32)]
    else:
        out_shape = [jax.ShapeDtypeStruct(own.shape, jnp.float32) for own, _, _ in parts]
    return pl.pallas_call(
        functools.partial(stencil_kernel, firsts, counts, strided),
        in_specs=[scalars] * 3 + [whole] * (1 + 3 * len(parts)),
        out_specs=[whole] * len(out_shape),
        out_shape=out_shape,
        compiler_params=pltpu.CompilerParams(vmem_limit_bytes=32 * 1024 * 1024),
        cost_estimate=pl.CostEstimate(flops=20 * cells, bytes_accessed=16 * cells, transcendentals=0),
        name="advance_strips" if strided else "advance_planes",
    )(place, params_a, params_b, source, *[x for part in parts for x in part])


def accumulate_kernel(counts, xb, *refs):
    n = len(counts)
    gathered = refs[:n]
    means_ref, squares_ref, cross_ref = refs[n : n + 3]
    new_means_ref, new_squares_ref, new_cross_ref, maps_ref = refs[n + 3 : n + 7]
    held = refs[n + 7]
    members = 10
    first = 0
    for g, count in zip(gathered, counts):
        for s in range(2):
            for mm in range(count):
                for h in range(2):
                    held[s * 5 + first + mm, pl.ds(h, xb, stride=2), :] = g[
                        s, pl.ds(mm * 2 + h, xb, stride=2 * count), :
                    ]
        first += count
    base = []
    for m in (0, 1):
        out, mean = held[m], means_ref[m]
        deviation = out - mean
        new_mean = mean + deviation / float(PRIOR + 1)
        after = out - new_mean
        new_square = squares_ref[m] + deviation * after
        new_means_ref[m] = new_mean
        new_squares_ref[m] = new_square
        base.append((deviation, new_square))
    for m in range(2, members):
        k = m - 2
        out, mean = held[m], means_ref[m]
        deviation = out - mean
        new_mean = mean + deviation / float(PRIOR + 1)
        after = out - new_mean
        new_square = squares_ref[m] + deviation * after
        new_means_ref[m] = new_mean
        new_squares_ref[m] = new_square
        first_cross = cross_ref[k] + base[1][0] * after
        total_cross = cross_ref[8 + k] + base[0][0] * after
        new_cross_ref[k] = first_cross
        new_cross_ref[8 + k] = total_cross
        maps_ref[k] = first_cross * lax.rsqrt(base[1][1] * new_square)
        maps_ref[8 + k] = 1.0 - total_cross * lax.rsqrt(base[0][1] * new_square)


def accumulate(gathered, counts, means, squares, cross):
    xb = 32
    nx = 128
    block = lambda lead: pl.BlockSpec((lead, 2 * xb, 128), lambda i: (0, i, 0))
    shape = lambda lead: jax.ShapeDtypeStruct((lead, 2 * nx, 128), jnp.float32)
    return pl.pallas_call(
        functools.partial(accumulate_kernel, counts, xb),
        grid=(nx // xb,),
        in_specs=[pl.BlockSpec((2, xb * 2 * count, 128), lambda i: (0, i, 0)) for count in counts]
        + [block(10), block(10), block(16)],
        out_specs=[block(10), block(10), block(16), block(16)],
        out_shape=[shape(10), shape(10), shape(16), shape(16)],
        scratch_shapes=[pltpu.VMEM((10, 2 * xb, 128), jnp.float32)],
        compiler_params=pltpu.CompilerParams(vmem_limit_bytes=32 * 1024 * 1024),
        cost_estimate=pl.CostEstimate(
            flops=40 * 10 * nx * 256, bytes_accessed=13 * 1024 * 1024, transcendentals=16 * nx * 256
        ),
        name="accumulate",
    )(*gathered, means, squares, cross)


def routes(count):
    near = [(i, i ^ 1) for i in range(count)]
    far = [(i, i + 1) for i in range(1, count - 1, 2)]
    far += [(j, i) for i, j in far]
    return near, far


def body(fields, source_field, params_a, params_b, running_means, running_squares, running_cross):
    near_route, far_route = routes(lax.axis_size("brick"))
    place = jnp.stack([lax.axis_index("side"), lax.axis_index("brick") % 2]).astype(jnp.int32)
    fields = fields[:, 0]
    source = source_field[0]
    firsts = [sum(CHUNKS[:i]) for i in range(len(CHUNKS))]
    currents = [fields[f : f + n] for f, n in zip(firsts, CHUNKS)]
    halo = lambda c: (c, lax.ppermute(c, "brick", near_route), lax.ppermute(c, "brick", far_route))
    step = lambda parts, fs, last: advance(place, params_a, params_b, source, parts, fs, last)
    parts = [halo(c) for c in currents]
    currents = [step([part], [f], False)[0] for part, f in zip(parts, firsts)]
    (mine,) = step([halo(c) for c in currents], firsts, True)
    strips = lax.all_to_all(
        mine.reshape(256, 1, 5 * 256), ("side", "brick"), split_axis=0, concat_axis=0, tiled=True
    )
    gathered = [strips.reshape(2, 128 * 2 * 5, 128)]
    flat = lambda x: x.reshape(x.shape[0], 256, 128)
    outs = accumulate(
        gathered, (5,), flat(running_means), flat(running_squares), flat(running_cross)
    )
    return tuple(o.reshape(o.shape[0], 128, 1, 256) for o in outs)


def solution(mesh):
    strips = P(None, None, ("side", "brick"), None)
    return jax.shard_map(
        body,
        mesh=mesh,
        in_specs=(
            P("side", "brick", None, None),
            P("brick", None, None),
            P(),
            P(),
            strips,
            strips,
            strips,
        ),
        out_specs=(strips, strips, strips, strips),
        check_vma=False,
    )
```

```python
import functools

import jax
import jax.numpy as jnp
import numpy as np
from jax import lax
from jax.experimental import pallas as pl
from jax.experimental.pallas import tpu as pltpu
from jax.sharding import PartitionSpec as P

PRIOR = 3
LOWER = np.asarray((0.02, 0.02, 0.02, 0.01, 0.0, 0.0, 0.5, 0.0), np.float32)
UPPER = np.asarray((0.12, 0.12, 0.12, 0.06, 0.2, 1.0, 1.5, 0.1), np.float32)
WIDTH = UPPER - LOWER
ROWS = 64


def weights_of(table_ref, m):
    member = table_ref[16] + jnp.asarray(m, jnp.float32)
    values = []
    for k in range(8):
        from_b = (member == 1.0) | (member == float(k + 2))
        unit = jnp.where(from_b, table_ref[8 + k], table_ref[k])
        values.append(float(LOWER[k]) + float(WIDTH[k]) * unit)
    drift_1, drift_2, drift_3, diffusion, decay, amplitude, anisotropy, reaction = values
    along = diffusion * anisotropy
    before = drift_1 + diffusion
    near_w = jnp.where(table_ref[17] == 0.0, diffusion, before)
    far_w = jnp.where(table_ref[17] == 0.0, before, diffusion)
    own_w = 1.0 - drift_1 - drift_2 - drift_3 - decay - diffusion * (4.0 + 2.0 * anisotropy)
    return own_w, near_w, far_w, drift_2 + diffusion, diffusion, drift_3 + along, along, amplitude, reaction


def step_plane(shape, weights, load, near, rest, store):
    own_w, near_w, _, y_before_w, y_after_w, z_before_w, z_after_w, _, reaction = weights
    ny, nz = shape
    column = lax.broadcasted_iota(jnp.int32, (ROWS, nz), 1)
    zero = jnp.zeros((8, nz), jnp.float32)
    for r in range(0, ny, ROWS):
        c = load(r, ROWS)
        above = load(r - 8, 8) if r > 0 else zero
        below = load(r + ROWS, 8) if r + ROWS < ny else zero
        wide = jnp.concatenate([above, c, below], axis=0)
        y_before = pltpu.roll(wide, 1, 0)[8 : 8 + ROWS]
        y_after = pltpu.roll(wide, ROWS + 15, 0)[8 : 8 + ROWS]
        z_before = jnp.where(column == 0, 0.0, pltpu.roll(c, 1, 1))
        z_after = jnp.where(column == nz - 1, 0.0, pltpu.roll(c, nz - 1, 1))
        new = (
            c * (own_w - reaction * jnp.abs(c))
            + near_w * near(r, ROWS)
            + y_before_w * y_before
            + y_after_w * y_after
            + z_before_w * z_before
            + z_after_w * z_after
            + rest(r, ROWS)
        )
        store(r, new)


def reader(ref, *at):
    return lambda r, n: ref[(*at, slice(r, r + n), slice(None))]


def store_strips(out_ref, m, count, r, new):
    pieces = new.shape[1] // 128
    pitch = count * pieces
    for h in range(pieces):
        start = r * pitch + m * pieces + h
        out_ref[pl.ds(start, new.shape[0], stride=pitch), :] = new[:, h * 128 : (h + 1) * 128]


def send_kernel(
    table_ref, raw_ref, source_ref, near_source_ref, near_ref, out_ref, partial_ref, copy_ref, source_copy_ref
):
    m = pl.program_id(0)
    weights = weights_of(table_ref, m)
    far_w, amplitude = weights[2], weights[7]
    count, ny, nz = copy_ref.shape
    for r in range(0, ny, ROWS):
        raw = raw_ref[0, r : r + ROWS, :]
        rest = far_w * raw + amplitude * near_source_ref[r : r + ROWS, :]
        store_strips(out_ref, m, count, r, far_w * rest)
        copy_ref[m, r : r + ROWS, :] = raw

    def store(r, new):
        partial_ref[m, r : r + ROWS, :] = new

    rest = lambda r, n: amplitude * source_ref[r : r + n, :]
    step_plane((ny, nz), weights, reader(raw_ref, 0), reader(near_ref, m), rest, store)

    @pl.when(m == 0)
    def _():
        for r in range(0, ny, ROWS):
            source_copy_ref[r : r + ROWS, :] = source_ref[r : r + ROWS, :]


def first_kernel(table_ref, partial_ref, far_ref, *out_refs):
    first = 0
    ny = far_ref.shape[1]
    for out_ref in out_refs:

        def one_member(j, carry, out_ref=out_ref, first=first):
            m = first + j
            far_w = weights_of(table_ref, m)[2]
            for r in range(0, ny, ROWS):
                rows = slice(r, r + ROWS)
                out_ref[j, rows, :] = partial_ref[m, rows, :] + far_w * far_ref[m, rows, :]
            return carry

        lax.fori_loop(0, out_ref.shape[0], one_member, 0)
        first += out_ref.shape[0]


def far_kernel(table_ref, raw_ref, raw_far_ref, out_ref):
    inside = table_ref[18] > 0.0

    def one_member(m, carry):
        weights = weights_of(table_ref, m)
        far_w = weights[2]

        def store(r, new):
            out_ref[m, r : r + ROWS, :] = jnp.where(inside, far_w * new, 0.0)

        step_plane(raw_ref.shape[1:], weights, reader(raw_far_ref, m), reader(raw_ref, m), lambda r, n: 0.0, store)
        return carry

    lax.fori_loop(0, raw_ref.shape[0], one_member, 0)


def second_kernel(table_ref, source_ref, far_part_ref, *refs):
    out_ref = refs[-1]
    count, ny, nz = far_part_ref.shape
    first = 0
    for own_ref, near_ref in zip(refs[:-1:2], refs[1:-1:2]):

        def one_member(j, carry, own_ref=own_ref, near_ref=near_ref, first=first):
            m = first + j
            weights = weights_of(table_ref, m)
            amplitude = weights[7]
            rest = lambda r, n: far_part_ref[m, r : r + n, :] + amplitude * source_ref[r : r + n, :]
            step_plane(
                (ny, nz), weights, reader(own_ref, j), reader(near_ref, j), rest,
                lambda r, new: store_strips(out_ref, m, count, r, new),
            )
            return carry

        lax.fori_loop(0, own_ref.shape[0], one_member, 0)
        first += own_ref.shape[0]


def add_kernel(table_ref, first_ref, second_ref, out_ref):
    rows = 160

    def some_rows(i, carry):
        at = pl.ds(pl.multiple_of(i * rows, rows), rows)
        out_ref[at, :] = first_ref[at, :] + second_ref[at, :]
        return carry

    lax.fori_loop(0, out_ref.shape[0] // rows, some_rows, 0)


def call(kernel, name, table, arrays, out_shapes, cells, scratch=(), grid=(), in_specs=None):
    whole = pl.BlockSpec(memory_space=pltpu.VMEM)
    return pl.pallas_call(
        kernel,
        grid=grid,
        in_specs=[pl.BlockSpec(memory_space=pltpu.SMEM)] + (in_specs or [whole] * len(arrays)),
        out_specs=[whole] * len(out_shapes),
        out_shape=[jax.ShapeDtypeStruct(shape, jnp.float32) for shape in out_shapes],
        scratch_shapes=scratch,
        compiler_params=pltpu.CompilerParams(vmem_limit_bytes=32 * 1024 * 1024),
        cost_estimate=pl.CostEstimate(flops=cells // 64, bytes_accessed=cells // 64, transcendentals=0),
        name=name,
    )(table, *arrays)


def accumulate_kernel(count, xb, gathered, means_ref, squares_ref, cross_ref, *outs):
    new_means_ref, new_squares_ref, new_cross_ref, maps_ref, held = outs
    i = pl.program_id(0)
    rows = pl.ds(pl.multiple_of(i * 2 * xb, 2 * xb), 2 * xb)
    for s in range(2):
        for m in range(count):
            for h in range(2):
                held[s * count + m, pl.ds(h, xb, stride=2), :] = gathered[
                    s, pl.ds(i * (xb * 2 * count) + m * 2 + h, xb, stride=2 * count), :
                ]

    def moments(m):
        out, mean = held[m], means_ref[m, rows, :]
        deviation = out - mean
        new_mean = mean + deviation * (1.0 / (PRIOR + 1))
        after = out - new_mean
        new_square = squares_ref[m, rows, :] + deviation * after
        new_means_ref[m] = new_mean
        new_squares_ref[m] = new_square
        return deviation, after, new_square

    base = [moments(0), moments(1)]
    for m in range(2, 2 * count):
        k = m - 2
        _, after, new_square = moments(m)
        first_cross = cross_ref[k, rows, :] + base[1][0] * after
        total_cross = cross_ref[8 + k, rows, :] + base[0][0] * after
        new_cross_ref[k] = first_cross
        new_cross_ref[8 + k] = total_cross
        maps_ref[k] = first_cross * lax.rsqrt(base[1][2] * new_square)
        maps_ref[8 + k] = 1.0 - total_cross * lax.rsqrt(base[0][2] * new_square)


def accumulate(gathered, count, means, squares, cross):
    xb = 32
    nx = 128
    whole = pl.BlockSpec(memory_space=pltpu.VMEM)
    block = lambda lead: pl.BlockSpec((lead, 2 * xb, 128), lambda i: (0, i, 0))
    shape = lambda lead: jax.ShapeDtypeStruct((lead, 2 * nx, 128), jnp.float32)
    return pl.pallas_call(
        functools.partial(accumulate_kernel, count, xb),
        grid=(nx // xb,),
        in_specs=[whole] * 4,
        out_specs=[block(10), block(10), block(16), block(16)],
        out_shape=[shape(10), shape(10), shape(16), shape(16)],
        scratch_shapes=[pltpu.VMEM((10, 2 * xb, 128), jnp.float32)],
        compiler_params=pltpu.CompilerParams(vmem_limit_bytes=32 * 1024 * 1024),
        cost_estimate=pl.CostEstimate(
            flops=40 * 10 * nx * 256, bytes_accessed=13 * 1024 * 1024, transcendentals=16 * nx * 256
        ),
        name="accumulate",
    )(gathered, means, squares, cross)


def routes(count):
    near = [(i, i ^ 1) for i in range(count)]
    far = [(i, i + 1) for i in range(1, count - 1, 2)]
    far += [(j, i) for i, j in far]
    second = [(i, i + 2) for i in range(0, count - 2, 2)] + [(i, i - 2) for i in range(3, count, 2)]
    return near, far, second


def body(fields, source_field, params_a, params_b, running_means, running_squares, running_cross):
    bricks = lax.axis_size("brick")
    near_route, far_route, second_route = routes(bricks)
    brick = lax.axis_index("brick")
    count = fields.shape[0]
    inside = (brick > 0) & (brick < bricks - 1)
    place = jnp.stack([lax.axis_index("side") * count, brick & 1, inside.astype(brick.dtype)])
    table = jnp.concatenate([params_a, params_b, place.astype(jnp.float32)])
    raw = fields[:, 0]
    source = source_field[0]
    send = lambda x, route: lax.ppermute(x, "brick", route)
    ny, nz = source.shape
    near_source = send(source, near_route)
    far = send(raw, far_route)
    near = send(raw, near_route)
    plane = lambda index: pl.BlockSpec((1, ny, nz), index)
    flat_shape = (raw.size // 128, 128)
    flat_plane = pl.BlockSpec((ny, nz), lambda m: (0, 0))
    beyond, partial, raw, source = call(
        send_kernel, "send_planes", table, (raw, source, near_source, near),
        (flat_shape, raw.shape, raw.shape, source.shape), raw.size, grid=(count,),
        in_specs=[plane(lambda m: (m, 0, 0)), flat_plane, flat_plane, pl.BlockSpec(memory_space=pltpu.VMEM)],
    )
    beyond = send(beyond, second_route)
    half = (count + 1) // 2
    ahead = call(
        first_kernel, "first_step", table, (partial, far), ((half, ny, nz), (count - half, ny, nz)), raw.size
    )
    pairs = [x for piece in ahead for x in (piece, send(piece, near_route))]
    (far_part,) = call(far_kernel, "far_step", table, (raw, far), (raw.shape,), raw.size)
    (mine,) = call(second_kernel, "second_step", table, (source, far_part, *pairs), (flat_shape,), raw.size)
    (mine,) = call(add_kernel, "add_beyond", table, (mine, beyond), (flat_shape,), raw.size // 8)
    strips = lax.all_to_all(
        mine.reshape(256, 1, count * 256), ("side", "brick"), split_axis=0, concat_axis=0, tiled=True
    )
    gathered = strips.reshape(2, 128 * 2 * count, 128)
    flat = lambda x: x.reshape(x.shape[0], 256, 128)
    outs = accumulate(
        gathered, count, flat(running_means), flat(running_squares), flat(running_cross)
    )
    return tuple(o.reshape(o.shape[0], 128, 1, 256) for o in outs)


def solution(mesh):
    strips = P(None, None, ("side", "brick"), None)
    return jax.shard_map(
        body,
        mesh=mesh,
        in_specs=(
            P("side", "brick", None, None),
            P("brick", None, None),
            P(),
            P(),
            strips,
            strips,
            strips,
        ),
        out_specs=(strips, strips, strips, strips),
        check_vma=False,
    )
```

```python
import functools

import jax
import jax.numpy as jnp
import numpy as np
from jax import lax
from jax.experimental import pallas as pl
from jax.experimental.pallas import tpu as pltpu
from jax.sharding import PartitionSpec as P

PRIOR = 3
LOWER = np.asarray((0.02, 0.02, 0.02, 0.01, 0.0, 0.0, 0.5, 0.0), np.float32)
UPPER = np.asarray((0.12, 0.12, 0.12, 0.06, 0.2, 1.0, 1.5, 0.1), np.float32)
WIDTH = UPPER - LOWER
ROWS = 64


def weights_of(table_ref, m):
    member = table_ref[16] + jnp.asarray(m, jnp.float32)
    values = []
    for k in range(8):
        from_b = (member == 1.0) | (member == float(k + 2))
        unit = jnp.where(from_b, table_ref[8 + k], table_ref[k])
        values.append(float(LOWER[k]) + float(WIDTH[k]) * unit)
    drift_1, drift_2, drift_3, diffusion, decay, amplitude, anisotropy, reaction = values
    along = diffusion * anisotropy
    before = drift_1 + diffusion
    near_w = jnp.where(table_ref[17] == 0.0, diffusion, before)
    far_w = jnp.where(table_ref[17] == 0.0, before, diffusion)
    own_w = 1.0 - drift_1 - drift_2 - drift_3 - decay - diffusion * (4.0 + 2.0 * anisotropy)
    return own_w, near_w, far_w, drift_2 + diffusion, diffusion, drift_3 + along, along, amplitude, reaction


def step_plane(shape, weights, load, near, rest, store):
    own_w, near_w, _, y_before_w, y_after_w, z_before_w, z_after_w, _, reaction = weights
    ny, nz = shape
    column = lax.broadcasted_iota(jnp.int32, (ROWS, nz), 1)
    zero = jnp.zeros((8, nz), jnp.float32)
    for r in range(0, ny, ROWS):
        c = load(r, ROWS)
        above = load(r - 8, 8) if r > 0 else zero
        below = load(r + ROWS, 8) if r + ROWS < ny else zero
        wide = jnp.concatenate([above, c, below], axis=0)
        y_before = pltpu.roll(wide, 1, 0)[8 : 8 + ROWS]
        y_after = pltpu.roll(wide, ROWS + 15, 0)[8 : 8 + ROWS]
        z_before = jnp.where(column == 0, 0.0, pltpu.roll(c, 1, 1))
        z_after = jnp.where(column == nz - 1, 0.0, pltpu.roll(c, nz - 1, 1))
        new = (
            c * (own_w - reaction * jnp.abs(c))
            + near_w * near(r, ROWS)
            + y_before_w * y_before
            + y_after_w * y_after
            + z_before_w * z_before
            + z_after_w * z_after
            + rest(r, ROWS)
        )
        store(r, new)


def reader(ref, *at):
    return lambda r, n: ref[(*at, slice(r, r + n), slice(None))]


def store_strips(out_ref, m, count, r, new):
    pieces = new.shape[1] // 128
    pitch = count * pieces
    for h in range(pieces):
        start = r * pitch + m * pieces + h
        out_ref[pl.ds(start, new.shape[0], stride=pitch), :] = new[:, h * 128 : (h + 1) * 128]


def send_kernel(table_ref, source_ref, *refs):
    pieces, (out_ref, partial_ref, source_copy_ref) = refs[:-3], refs[-3:]
    count, ny, nz = partial_ref.shape
    for r in range(0, ny, ROWS):
        source_copy_ref[r : r + ROWS, :] = source_ref[r : r + ROWS, :]
    first = 0
    for raw_ref, near_ref in zip(pieces[::2], pieces[1::2]):

        def one_member(j, carry, raw_ref=raw_ref, near_ref=near_ref, first=first):
            m = first + j
            weights = weights_of(table_ref, m)
            near_w, amplitude = weights[1], weights[7]
            for r in range(0, ny, ROWS):
                rows = slice(r, r + ROWS)
                rest = near_w * near_ref[j, rows, :] + amplitude * source_ref[rows, :]
                store_strips(out_ref, m, count, r, near_w * rest)

            def store(r, new):
                partial_ref[m, r : r + ROWS, :] = new

            rest = lambda r, n: amplitude * source_ref[r : r + n, :]
            step_plane((ny, nz), weights, reader(raw_ref, j), reader(near_ref, j), rest, store)
            return carry

        lax.fori_loop(0, raw_ref.shape[0], one_member, 0)
        first += raw_ref.shape[0]


def first_kernel(table_ref, partial_ref, far_ref, *out_refs):
    first = 0
    ny = far_ref.shape[1]
    for out_ref in out_refs:

        def one_member(j, carry, out_ref=out_ref, first=first):
            m = first + j
            far_w = weights_of(table_ref, m)[2]
            for r in range(0, ny, ROWS):
                rows = slice(r, r + ROWS)
                out_ref[j, rows, :] = partial_ref[m, rows, :] + far_w * far_ref[m, rows, :]
            return carry

        lax.fori_loop(0, out_ref.shape[0], one_member, 0)
        first += out_ref.shape[0]


def far_kernel(table_ref, raw_far_ref, *refs):
    pieces, out_ref = refs[:-1], refs[-1]
    inside = table_ref[18] > 0.0
    first = 0
    for raw_ref in pieces:

        def one_member(j, carry, raw_ref=raw_ref, first=first):
            m = first + j
            weights = weights_of(table_ref, m)
            far_w = weights[2]

            def store(r, new):
                out_ref[m, r : r + ROWS, :] = jnp.where(inside, far_w * new, 0.0)

            step_plane(
                out_ref.shape[1:], weights, reader(raw_far_ref, m), reader(raw_ref, j), lambda r, n: 0.0, store
            )
            return carry

        lax.fori_loop(0, raw_ref.shape[0], one_member, 0)
        first += raw_ref.shape[0]


def second_kernel(table_ref, source_ref, far_part_ref, *refs):
    out_ref = refs[-1]
    count, ny, nz = far_part_ref.shape
    first = 0
    for own_ref, near_ref in zip(refs[:-1:2], refs[1:-1:2]):

        def one_member(j, carry, own_ref=own_ref, near_ref=near_ref, first=first):
            m = first + j
            weights = weights_of(table_ref, m)
            amplitude = weights[7]
            rest = lambda r, n: far_part_ref[m, r : r + n, :] + amplitude * source_ref[r : r + n, :]
            step_plane(
                (ny, nz), weights, reader(own_ref, j), reader(near_ref, j), rest,
                lambda r, new: store_strips(out_ref, m, count, r, new),
            )
            return carry

        lax.fori_loop(0, own_ref.shape[0], one_member, 0)
        first += own_ref.shape[0]


def add_kernel(table_ref, first_ref, second_ref, out_ref):
    rows = 160

    def some_rows(i, carry):
        at = pl.ds(pl.multiple_of(i * rows, rows), rows)
        out_ref[at, :] = first_ref[at, :] + second_ref[at, :]
        return carry

    lax.fori_loop(0, out_ref.shape[0] // rows, some_rows, 0)


def call(kernel, name, table, arrays, out_shapes, cells):
    whole = pl.BlockSpec(memory_space=pltpu.VMEM)
    return pl.pallas_call(
        kernel,
        in_specs=[pl.BlockSpec(memory_space=pltpu.SMEM)] + [whole] * len(arrays),
        out_specs=[whole] * len(out_shapes),
        out_shape=[jax.ShapeDtypeStruct(shape, jnp.float32) for shape in out_shapes],
        compiler_params=pltpu.CompilerParams(vmem_limit_bytes=32 * 1024 * 1024),
        cost_estimate=pl.CostEstimate(flops=cells // 64, bytes_accessed=cells // 64, transcendentals=0),
        name=name,
    )(table, *arrays)


def accumulate_kernel(count, xb, gathered, means_ref, squares_ref, cross_ref, *outs):
    new_means_ref, new_squares_ref, new_cross_ref, maps_ref, held = outs
    i = pl.program_id(0)
    rows = pl.ds(pl.multiple_of(i * 2 * xb, 2 * xb), 2 * xb)
    for s in range(2):
        for m in range(count):
            for h in range(2):
                held[s * count + m, pl.ds(h, xb, stride=2), :] = gathered[
                    s, pl.ds(i * (xb * 2 * count) + m * 2 + h, xb, stride=2 * count), :
                ]

    def moments(m):
        out, mean = held[m], means_ref[m, rows, :]
        deviation = out - mean
        new_mean = mean + deviation * (1.0 / (PRIOR + 1))
        after = out - new_mean
        new_square = squares_ref[m, rows, :] + deviation * after
        new_means_ref[m] = new_mean
        new_squares_ref[m] = new_square
        return deviation, after, new_square

    base = [moments(0), moments(1)]
    for m in range(2, 2 * count):
        k = m - 2
        _, after, new_square = moments(m)
        first_cross = cross_ref[k, rows, :] + base[1][0] * after
        total_cross = cross_ref[8 + k, rows, :] + base[0][0] * after
        new_cross_ref[k] = first_cross
        new_cross_ref[8 + k] = total_cross
        maps_ref[k] = first_cross * lax.rsqrt(base[1][2] * new_square)
        maps_ref[8 + k] = 1.0 - total_cross * lax.rsqrt(base[0][2] * new_square)


def accumulate(gathered, count, means, squares, cross):
    xb = 32
    nx = 128
    whole = pl.BlockSpec(memory_space=pltpu.VMEM)
    block = lambda lead: pl.BlockSpec((lead, 2 * xb, 128), lambda i: (0, i, 0))
    shape = lambda lead: jax.ShapeDtypeStruct((lead, 2 * nx, 128), jnp.float32)
    return pl.pallas_call(
        functools.partial(accumulate_kernel, count, xb),
        grid=(nx // xb,),
        in_specs=[whole] * 4,
        out_specs=[block(10), block(10), block(16), block(16)],
        out_shape=[shape(10), shape(10), shape(16), shape(16)],
        scratch_shapes=[pltpu.VMEM((10, 2 * xb, 128), jnp.float32)],
        compiler_params=pltpu.CompilerParams(vmem_limit_bytes=32 * 1024 * 1024),
        cost_estimate=pl.CostEstimate(
            flops=40 * 10 * nx * 256, bytes_accessed=13 * 1024 * 1024, transcendentals=16 * nx * 256
        ),
        name="accumulate",
    )(gathered, means, squares, cross)


def routes(count):
    near = [(i, i ^ 1) for i in range(count)]
    far = [(i, i + 1) for i in range(1, count - 1, 2)]
    far += [(j, i) for i, j in far]
    return near, far


def body(fields, source_field, params_a, params_b, running_means, running_squares, running_cross):
    bricks = lax.axis_size("brick")
    near_route, far_route = routes(bricks)
    brick = lax.axis_index("brick")
    count = fields.shape[0]
    inside = (brick > 0) & (brick < bricks - 1)
    place = jnp.stack([lax.axis_index("side") * count, brick & 1, inside.astype(brick.dtype)])
    table = jnp.concatenate([params_a, params_b, place.astype(jnp.float32)])
    raw = fields[:, 0]
    source = source_field[0]
    send = lambda x, route: lax.ppermute(x, "brick", route)
    ny, nz = source.shape
    half = (count + 1) // 2
    halves = (raw[:half], raw[half:])
    flat_shape = (raw.size // 128, 128)
    far = send(raw, far_route)
    pairs = [x for piece in halves for x in (piece, send(piece, near_route))]
    beyond, partial, source = call(
        send_kernel, "send_planes", table, (source, *pairs), (flat_shape, raw.shape, source.shape), raw.size
    )
    beyond = send(beyond, far_route)
    ahead = call(
        first_kernel, "first_step", table, (partial, far), [piece.shape for piece in halves], raw.size
    )
    pairs = [x for piece in ahead for x in (piece, send(piece, near_route))]
    (far_part,) = call(far_kernel, "far_step", table, (far, *halves), (raw.shape,), raw.size)
    (mine,) = call(second_kernel, "second_step", table, (source, far_part, *pairs), (flat_shape,), raw.size)
    (mine,) = call(add_kernel, "add_beyond", table, (mine, beyond), (flat_shape,), raw.size // 8)
    strips = lax.all_to_all(
        mine.reshape(256, 1, count * 256), ("side", "brick"), split_axis=0, concat_axis=0, tiled=True
    )
    gathered = strips.reshape(2, 128 * 2 * count, 128)
    flat = lambda x: x.reshape(x.shape[0], 256, 128)
    outs = accumulate(
        gathered, count, flat(running_means), flat(running_squares), flat(running_cross)
    )
    return tuple(o.reshape(o.shape[0], 128, 1, 256) for o in outs)


def solution(mesh):
    strips = P(None, None, ("side", "brick"), None)
    return jax.shard_map(
        body,
        mesh=mesh,
        in_specs=(
            P("side", "brick", None, None),
            P("brick", None, None),
            P(),
            P(),
            strips,
            strips,
            strips,
        ),
        out_specs=(strips, strips, strips, strips),
        check_vma=False,
    )
```

```python
import functools

import jax
import jax.numpy as jnp
import numpy as np
from jax import lax
from jax.experimental import pallas as pl
from jax.experimental.pallas import tpu as pltpu
from jax.sharding import PartitionSpec as P

PRIOR = 3
LOWER = np.asarray((0.02, 0.02, 0.02, 0.01, 0.0, 0.0, 0.5, 0.0), np.float32)
UPPER = np.asarray((0.12, 0.12, 0.12, 0.06, 0.2, 1.0, 1.5, 0.1), np.float32)
WIDTH = UPPER - LOWER
ROWS = 64
LAST = 64


def weights_of(table_ref, m):
    member = table_ref[16] + jnp.asarray(m, jnp.float32)
    values = []
    for k in range(8):
        from_b = (member == 1.0) | (member == float(k + 2))
        unit = jnp.where(from_b, table_ref[8 + k], table_ref[k])
        values.append(float(LOWER[k]) + float(WIDTH[k]) * unit)
    drift_1, drift_2, drift_3, diffusion, decay, amplitude, anisotropy, reaction = values
    along = diffusion * anisotropy
    before = drift_1 + diffusion
    near_w = jnp.where(table_ref[17] == 0.0, diffusion, before)
    far_w = jnp.where(table_ref[17] == 0.0, before, diffusion)
    own_w = 1.0 - drift_1 - drift_2 - drift_3 - decay - diffusion * (4.0 + 2.0 * anisotropy)
    return own_w, near_w, far_w, drift_2 + diffusion, diffusion, drift_3 + along, along, amplitude, reaction


def step_plane(shape, weights, load, near, rest, store):
    own_w, near_w, _, y_before_w, y_after_w, z_before_w, z_after_w, _, reaction = weights
    ny, nz = shape
    column = lax.broadcasted_iota(jnp.int32, (ROWS, nz), 1)
    zero = jnp.zeros((8, nz), jnp.float32)
    for r in range(0, ny, ROWS):
        c = load(r, ROWS)
        above = load(r - 8, 8) if r > 0 else zero
        below = load(r + ROWS, 8) if r + ROWS < ny else zero
        wide = jnp.concatenate([above, c, below], axis=0)
        y_before = pltpu.roll(wide, 1, 0)[8 : 8 + ROWS]
        y_after = pltpu.roll(wide, ROWS + 15, 0)[8 : 8 + ROWS]
        z_before = jnp.where(column == 0, 0.0, pltpu.roll(c, 1, 1))
        z_after = jnp.where(column == nz - 1, 0.0, pltpu.roll(c, nz - 1, 1))
        new = (
            c * (own_w - reaction * jnp.abs(c))
            + near_w * near(r, ROWS)
            + y_before_w * y_before
            + y_after_w * y_after
            + z_before_w * z_before
            + z_after_w * z_after
            + rest(r, ROWS)
        )
        store(r, new)


def reader(ref, *at):
    return lambda r, n: ref[(*at, slice(r, r + n), slice(None))]


def store_strips(out_ref, m, count, r, new):
    pieces = new.shape[1] // 128
    pitch = count * pieces
    for h in range(pieces):
        start = r * pitch + m * pieces + h
        out_ref[pl.ds(start, new.shape[0], stride=pitch), :] = new[:, h * 128 : (h + 1) * 128]


def send_kernel(table_ref, source_ref, *refs):
    pieces, (out_ref, last_ref, partial_ref, source_copy_ref) = refs[:-4], refs[-4:]
    count, ny, nz = partial_ref.shape
    for r in range(0, ny, ROWS):
        source_copy_ref[r : r + ROWS, :] = source_ref[r : r + ROWS, :]
    first = 0
    for raw_ref, near_ref in zip(pieces[::2], pieces[1::2]):

        def one_member(j, carry, raw_ref=raw_ref, near_ref=near_ref, first=first):
            m = first + j
            weights = weights_of(table_ref, m)
            near_w, amplitude = weights[1], weights[7]
            for r in range(0, ny, ROWS):
                rows = slice(r, r + ROWS)
                rest = near_w * near_ref[j, rows, :] + amplitude * source_ref[rows, :]
                if r < ny - LAST:
                    store_strips(out_ref, m, count, r, near_w * rest)
                else:
                    store_strips(last_ref, m, count, r - (ny - LAST), near_w * rest)

            def store(r, new):
                partial_ref[m, r : r + ROWS, :] = new

            rest = lambda r, n: amplitude * source_ref[r : r + n, :]
            step_plane((ny, nz), weights, reader(raw_ref, j), reader(near_ref, j), rest, store)
            return carry

        lax.fori_loop(0, raw_ref.shape[0], one_member, 0)
        first += raw_ref.shape[0]


def first_kernel(table_ref, partial_ref, far_ref, *out_refs):
    first = 0
    ny = far_ref.shape[1]
    for out_ref in out_refs:

        def one_member(j, carry, out_ref=out_ref, first=first):
            m = first + j
            far_w = weights_of(table_ref, m)[2]
            for r in range(0, ny, ROWS):
                rows = slice(r, r + ROWS)
                out_ref[j, rows, :] = partial_ref[m, rows, :] + far_w * far_ref[m, rows, :]
            return carry

        lax.fori_loop(0, out_ref.shape[0], one_member, 0)
        first += out_ref.shape[0]


def far_kernel(table_ref, raw_far_ref, *refs):
    pieces, out_ref = refs[:-1], refs[-1]
    inside = table_ref[18] > 0.0
    first = 0
    for raw_ref in pieces:

        def one_member(j, carry, raw_ref=raw_ref, first=first):
            m = first + j
            weights = weights_of(table_ref, m)
            far_w = weights[2]

            def store(r, new):
                out_ref[m, r : r + ROWS, :] = jnp.where(inside, far_w * new, 0.0)

            step_plane(
                out_ref.shape[1:], weights, reader(raw_far_ref, m), reader(raw_ref, j), lambda r, n: 0.0, store
            )
            return carry

        lax.fori_loop(0, raw_ref.shape[0], one_member, 0)
        first += raw_ref.shape[0]


def second_kernel(table_ref, source_ref, far_part_ref, *refs):
    out_ref = refs[-1]
    count, ny, nz = far_part_ref.shape
    first = 0
    for own_ref, near_ref in zip(refs[:-1:2], refs[1:-1:2]):

        def one_member(j, carry, own_ref=own_ref, near_ref=near_ref, first=first):
            m = first + j
            weights = weights_of(table_ref, m)
            amplitude = weights[7]
            rest = lambda r, n: far_part_ref[m, r : r + n, :] + amplitude * source_ref[r : r + n, :]
            step_plane(
                (ny, nz), weights, reader(own_ref, j), reader(near_ref, j), rest,
                lambda r, new: store_strips(out_ref, m, count, r, new),
            )
            return carry

        lax.fori_loop(0, own_ref.shape[0], one_member, 0)
        first += own_ref.shape[0]


def add_kernel(first, table_ref, into_ref, part_ref, out_ref):
    rows = 320

    def some_rows(i, carry):
        start = pl.multiple_of(i * rows, rows)
        at = pl.ds(first + start, rows)
        out_ref[at, :] = into_ref[at, :] + part_ref[pl.ds(start, rows), :]
        return carry

    lax.fori_loop(0, part_ref.shape[0] // rows, some_rows, 0)


def call(kernel, name, table, arrays, out_shapes, cells, aliases={}):
    whole = pl.BlockSpec(memory_space=pltpu.VMEM)
    return pl.pallas_call(
        kernel,
        in_specs=[pl.BlockSpec(memory_space=pltpu.SMEM)] + [whole] * len(arrays),
        out_specs=[whole] * len(out_shapes),
        out_shape=[jax.ShapeDtypeStruct(shape, jnp.float32) for shape in out_shapes],
        input_output_aliases=aliases,
        compiler_params=pltpu.CompilerParams(vmem_limit_bytes=32 * 1024 * 1024),
        cost_estimate=pl.CostEstimate(flops=cells // 64, bytes_accessed=cells // 64, transcendentals=0),
        name=name,
    )(table, *arrays)


def accumulate_kernel(count, xb, gathered, means_ref, squares_ref, cross_ref, *refs):
    outs, blocks, (held, copied) = refs[:4], refs[4:8], refs[8:]
    new_means_ref, new_squares_ref, new_cross_ref, maps_ref = blocks
    copies = []
    for i in range(128 // xb):
        rows = pl.ds(i * 2 * xb, 2 * xb)
        for s in range(2):
            for m in range(count):
                for h in range(2):
                    held[s * count + m, pl.ds(h, xb, stride=2), :] = gathered[
                        s, pl.ds(i * (xb * 2 * count) + m * 2 + h, xb, stride=2 * count), :
                    ]

        def moments(m):
            out, mean = held[m], means_ref[m, rows, :]
            deviation = out - mean
            new_mean = mean + deviation * (1.0 / (PRIOR + 1))
            after = out - new_mean
            new_square = squares_ref[m, rows, :] + deviation * after
            new_means_ref[m, rows, :] = new_mean
            new_squares_ref[m, rows, :] = new_square
            return deviation, after, new_square

        base = [moments(0), moments(1)]
        for m in range(2, 2 * count):
            k = m - 2
            _, after, new_square = moments(m)
            first_cross = cross_ref[k, rows, :] + base[1][0] * after
            total_cross = cross_ref[8 + k, rows, :] + base[0][0] * after
            new_cross_ref[k, rows, :] = first_cross
            new_cross_ref[8 + k, rows, :] = total_cross
            maps_ref[k, rows, :] = first_cross * lax.rsqrt(base[1][2] * new_square)
            maps_ref[8 + k, rows, :] = 1.0 - total_cross * lax.rsqrt(base[0][2] * new_square)
        for j, (block, out) in enumerate(zip(blocks, outs)):
            copy = pltpu.make_async_copy(block.at[:, rows], out.at[:, rows], copied.at[i, j])
            copy.start()
            copies.append(copy)
    for copy in copies:
        copy.wait()


def accumulate(gathered, count, means, squares, cross):
    xb = 32
    nx = 128
    whole = pl.BlockSpec(memory_space=pltpu.VMEM)
    shape = lambda lead: (lead, 2 * nx, 128)
    leads = (10, 10, 16, 16)
    return pl.pallas_call(
        functools.partial(accumulate_kernel, count, xb),
        in_specs=[whole] * 4,
        out_specs=[pl.BlockSpec(memory_space=pl.ANY)] * 4,
        out_shape=[jax.ShapeDtypeStruct(shape(lead), jnp.float32) for lead in leads],
        scratch_shapes=[pltpu.VMEM(shape(lead), jnp.float32) for lead in leads]
        + [pltpu.VMEM((10, 2 * xb, 128), jnp.float32), pltpu.SemaphoreType.DMA((nx // xb, 4))],
        compiler_params=pltpu.CompilerParams(vmem_limit_bytes=32 * 1024 * 1024),
        cost_estimate=pl.CostEstimate(
            flops=40 * 10 * nx * 256, bytes_accessed=13 * 1024 * 1024, transcendentals=16 * nx * 256
        ),
        name="accumulate",
    )(gathered, means, squares, cross)


def routes(count):
    near = [(i, i ^ 1) for i in range(count)]
    far = [(i, i + 1) for i in range(1, count - 1, 2)]
    far += [(j, i) for i, j in far]
    return near, far


def body(fields, source_field, params_a, params_b, running_means, running_squares, running_cross):
    bricks = lax.axis_size("brick")
    near_route, far_route = routes(bricks)
    brick = lax.axis_index("brick")
    count = fields.shape[0]
    inside = (brick > 0) & (brick < bricks - 1)
    place = jnp.stack([lax.axis_index("side") * count, brick & 1, inside.astype(brick.dtype)])
    table = jnp.concatenate([params_a, params_b, place.astype(jnp.float32)])
    raw = fields[:, 0]
    source = source_field[0]
    send = lambda x, route: lax.ppermute(x, "brick", route)
    ny, nz = source.shape
    half = (count + 1) // 2
    halves = (raw[:half], raw[half:])
    flat_shape = (raw.size // 128, 128)
    far = send(raw, far_route)
    pairs = [x for piece in halves for x in (piece, send(piece, near_route))]
    cut = (ny - LAST) * count * (nz // 128)
    *beyond, partial, source = call(
        send_kernel, "send_planes", table, (source, *pairs),
        ((cut, 128), (raw.size // 128 - cut, 128), raw.shape, source.shape), raw.size,
    )
    beyond = [send(part, far_route) for part in beyond]
    ahead = call(
        first_kernel, "first_step", table, (partial, far), [piece.shape for piece in halves], raw.size
    )
    pairs = [x for piece in ahead for x in (piece, send(piece, near_route))]
    (far_part,) = call(far_kernel, "far_step", table, (far, *halves), (raw.shape,), raw.size)
    (mine,) = call(second_kernel, "second_step", table, (source, far_part, *pairs), (flat_shape,), raw.size)
    for start, part in zip((0, cut), beyond):
        (mine,) = call(
            functools.partial(add_kernel, start), "add_beyond", table, (mine, part), (flat_shape,), part.size // 8,
            aliases={1: 0},
        )
    strips = lax.all_to_all(
        mine.reshape(256, 1, count * 256), ("side", "brick"), split_axis=0, concat_axis=0, tiled=True
    )
    gathered = strips.reshape(2, 128 * 2 * count, 128)
    flat = lambda x: x.reshape(x.shape[0], 256, 128)
    outs = accumulate(
        gathered, count, flat(running_means), flat(running_squares), flat(running_cross)
    )
    return tuple(o.reshape(o.shape[0], 128, 1, 256) for o in outs)


def solution(mesh):
    strips = P(None, None, ("side", "brick"), None)
    return jax.shard_map(
        body,
        mesh=mesh,
        in_specs=(
            P("side", "brick", None, None),
            P("brick", None, None),
            P(),
            P(),
            strips,
            strips,
            strips,
        ),
        out_specs=(strips, strips, strips, strips),
        check_vma=False,
    )
```

```python
import functools

import jax
import jax.numpy as jnp
import numpy as np
from jax import lax
from jax.experimental import pallas as pl
from jax.experimental.pallas import tpu as pltpu
from jax.sharding import PartitionSpec as P

PRIOR = 3
LOWER = np.asarray((0.02, 0.02, 0.02, 0.01, 0.0, 0.0, 0.5, 0.0), np.float32)
UPPER = np.asarray((0.12, 0.12, 0.12, 0.06, 0.2, 1.0, 1.5, 0.1), np.float32)
WIDTH = UPPER - LOWER
ROWS = 64


def weights_of(table_ref, m):
    member = table_ref[16] + jnp.asarray(m, jnp.float32)
    values = []
    for k in range(8):
        from_b = (member == 1.0) | (member == float(k + 2))
        unit = jnp.where(from_b, table_ref[8 + k], table_ref[k])
        values.append(float(LOWER[k]) + float(WIDTH[k]) * unit)
    drift_1, drift_2, drift_3, diffusion, decay, amplitude, anisotropy, reaction = values
    along = diffusion * anisotropy
    before = drift_1 + diffusion
    near_w = jnp.where(table_ref[17] == 0.0, diffusion, before)
    far_w = jnp.where(table_ref[17] == 0.0, before, diffusion)
    own_w = 1.0 - drift_1 - drift_2 - drift_3 - decay - diffusion * (4.0 + 2.0 * anisotropy)
    return own_w, near_w, far_w, drift_2 + diffusion, diffusion, drift_3 + along, along, amplitude, reaction


def step_plane(shape, weights, load, near, rest, store):
    own_w, near_w, _, y_before_w, y_after_w, z_before_w, z_after_w, _, reaction = weights
    ny, nz = shape
    column = lax.broadcasted_iota(jnp.int32, (ROWS, nz), 1)
    zero = jnp.zeros((8, nz), jnp.float32)
    for r in range(0, ny, ROWS):
        c = load(r, ROWS)
        above = load(r - 8, 8) if r > 0 else zero
        below = load(r + ROWS, 8) if r + ROWS < ny else zero
        wide = jnp.concatenate([above, c, below], axis=0)
        y_before = pltpu.roll(wide, 1, 0)[8 : 8 + ROWS]
        y_after = pltpu.roll(wide, ROWS + 15, 0)[8 : 8 + ROWS]
        z_before = jnp.where(column == 0, 0.0, pltpu.roll(c, 1, 1))
        z_after = jnp.where(column == nz - 1, 0.0, pltpu.roll(c, nz - 1, 1))
        new = (
            c * (own_w - reaction * jnp.abs(c))
            + near_w * near(r, ROWS)
            + y_before_w * y_before
            + y_after_w * y_after
            + z_before_w * z_before
            + z_after_w * z_after
            + rest(r, ROWS)
        )
        store(r, new)


def reader(ref, *at):
    return lambda r, n: ref[(*at, slice(r, r + n), slice(None))]


def store_strips(out_ref, m, count, r, new):
    pieces = new.shape[1] // 128
    pitch = count * pieces
    for h in range(pieces):
        start = r * pitch + m * pieces + h
        out_ref[pl.ds(start, new.shape[0], stride=pitch), :] = new[:, h * 128 : (h + 1) * 128]


def send_kernel(table_ref, source_ref, *refs):
    pieces, (out_ref, partial_ref, source_copy_ref) = refs[:-3], refs[-3:]
    count, ny, nz = partial_ref.shape
    for r in range(0, ny, ROWS):
        source_copy_ref[r : r + ROWS, :] = source_ref[r : r + ROWS, :]
    first = 0
    for raw_ref, near_ref in zip(pieces[::2], pieces[1::2]):

        def one_member(j, carry, raw_ref=raw_ref, near_ref=near_ref, first=first):
            m = first + j
            weights = weights_of(table_ref, m)
            near_w, amplitude = weights[1], weights[7]
            for r in range(0, ny, ROWS):
                rows = slice(r, r + ROWS)
                rest = near_w * near_ref[j, rows, :] + amplitude * source_ref[rows, :]
                store_strips(out_ref, m, count, r, near_w * rest)

            def store(r, new):
                partial_ref[m, r : r + ROWS, :] = new

            rest = lambda r, n: amplitude * source_ref[r : r + n, :]
            step_plane((ny, nz), weights, reader(raw_ref, j), reader(near_ref, j), rest, store)
            return carry

        lax.fori_loop(0, raw_ref.shape[0], one_member, 0)
        first += raw_ref.shape[0]


def first_kernel(table_ref, partial_ref, far_ref, *out_refs):
    first = 0
    ny = far_ref.shape[1]
    for out_ref in out_refs:

        def one_member(j, carry, out_ref=out_ref, first=first):
            m = first + j
            far_w = weights_of(table_ref, m)[2]
            for r in range(0, ny, ROWS):
                rows = slice(r, r + ROWS)
                out_ref[j, rows, :] = partial_ref[m, rows, :] + far_w * far_ref[m, rows, :]
            return carry

        lax.fori_loop(0, out_ref.shape[0], one_member, 0)
        first += out_ref.shape[0]


def far_kernel(table_ref, raw_far_ref, *refs):
    pieces, out_ref = refs[:-1], refs[-1]
    inside = table_ref[18] > 0.0
    first = 0
    for raw_ref in pieces:

        def one_member(j, carry, raw_ref=raw_ref, first=first):
            m = first + j
            weights = weights_of(table_ref, m)
            far_w = weights[2]

            def store(r, new):
                out_ref[m, r : r + ROWS, :] = jnp.where(inside, far_w * new, 0.0)

            step_plane(
                out_ref.shape[1:], weights, reader(raw_far_ref, m), reader(raw_ref, j), lambda r, n: 0.0, store
            )
            return carry

        lax.fori_loop(0, raw_ref.shape[0], one_member, 0)
        first += raw_ref.shape[0]


def second_kernel(table_ref, source_ref, far_part_ref, *refs):
    out_ref = refs[-1]
    count, ny, nz = far_part_ref.shape
    first = 0
    for own_ref, near_ref in zip(refs[:-1:2], refs[1:-1:2]):

        def one_member(j, carry, own_ref=own_ref, near_ref=near_ref, first=first):
            m = first + j
            weights = weights_of(table_ref, m)
            amplitude = weights[7]
            rest = lambda r, n: far_part_ref[m, r : r + n, :] + amplitude * source_ref[r : r + n, :]
            step_plane(
                (ny, nz), weights, reader(own_ref, j), reader(near_ref, j), rest,
                lambda r, new: store_strips(out_ref, m, count, r, new),
            )
            return carry

        lax.fori_loop(0, own_ref.shape[0], one_member, 0)
        first += own_ref.shape[0]


def add_kernel(first_ref, second_ref, out_ref):
    rows = 320

    def some_rows(i, carry):
        at = pl.ds(pl.multiple_of(i * rows, rows), rows)
        out_ref[at, :] = first_ref[at, :] + second_ref[at, :]
        return carry

    lax.fori_loop(0, out_ref.shape[0] // rows, some_rows, 0)


def call(kernel, name, scalars, arrays, out_shapes, cells):
    whole = pl.BlockSpec(memory_space=pltpu.VMEM)
    return pl.pallas_call(
        kernel,
        in_specs=[pl.BlockSpec(memory_space=pltpu.SMEM)] * len(scalars) + [whole] * len(arrays),
        out_specs=[whole] * len(out_shapes),
        out_shape=[jax.ShapeDtypeStruct(shape, jnp.float32) for shape in out_shapes],
        compiler_params=pltpu.CompilerParams(vmem_limit_bytes=32 * 1024 * 1024),
        cost_estimate=pl.CostEstimate(flops=cells // 64, bytes_accessed=cells // 64, transcendentals=0),
        name=name,
    )(*scalars, *arrays)


def accumulate_kernel(count, xb, gathered, means_ref, squares_ref, cross_ref, *refs):
    outs, blocks, (held, copied) = refs[:4], refs[4:8], refs[8:]
    new_means_ref, new_squares_ref, new_cross_ref, maps_ref = blocks
    copies = []
    for i in range(128 // xb):
        rows = pl.ds(i * 2 * xb, 2 * xb)
        for s in range(2):
            for m in range(count):
                for h in range(2):
                    held[s * count + m, pl.ds(h, xb, stride=2), :] = gathered[
                        s, pl.ds(i * (xb * 2 * count) + m * 2 + h, xb, stride=2 * count), :
                    ]

        def moments(m):
            out, mean = held[m], means_ref[m, rows, :]
            deviation = out - mean
            new_mean = mean + deviation * (1.0 / (PRIOR + 1))
            after = out - new_mean
            new_square = squares_ref[m, rows, :] + deviation * after
            new_means_ref[m, rows, :] = new_mean
            new_squares_ref[m, rows, :] = new_square
            return deviation, after, new_square

        base = [moments(0), moments(1)]
        for m in range(2, 2 * count):
            k = m - 2
            _, after, new_square = moments(m)
            first_cross = cross_ref[k, rows, :] + base[1][0] * after
            total_cross = cross_ref[8 + k, rows, :] + base[0][0] * after
            new_cross_ref[k, rows, :] = first_cross
            new_cross_ref[8 + k, rows, :] = total_cross
            maps_ref[k, rows, :] = first_cross * lax.rsqrt(base[1][2] * new_square)
            maps_ref[8 + k, rows, :] = 1.0 - total_cross * lax.rsqrt(base[0][2] * new_square)
        for j, (block, out) in enumerate(zip(blocks, outs)):
            copy = pltpu.make_async_copy(block.at[:, rows], out.at[:, rows], copied.at[i, j])
            copy.start()
            copies.append(copy)
    for copy in copies:
        copy.wait()


def accumulate(gathered, count, means, squares, cross):
    xb = 32
    nx = 128
    whole = pl.BlockSpec(memory_space=pltpu.VMEM)
    shape = lambda lead: (lead, 2 * nx, 128)
    leads = (10, 10, 16, 16)
    return pl.pallas_call(
        functools.partial(accumulate_kernel, count, xb),
        in_specs=[whole] * 4,
        out_specs=[pl.BlockSpec(memory_space=pl.ANY)] * 4,
        out_shape=[jax.ShapeDtypeStruct(shape(lead), jnp.float32) for lead in leads],
        scratch_shapes=[pltpu.VMEM(shape(lead), jnp.float32) for lead in leads]
        + [pltpu.VMEM((10, 2 * xb, 128), jnp.float32), pltpu.SemaphoreType.DMA((nx // xb, 4))],
        compiler_params=pltpu.CompilerParams(vmem_limit_bytes=32 * 1024 * 1024),
        cost_estimate=pl.CostEstimate(
            flops=40 * 10 * nx * 256, bytes_accessed=13 * 1024 * 1024, transcendentals=16 * nx * 256
        ),
        name="accumulate",
    )(gathered, means, squares, cross)


def routes(count):
    near = [(i, i ^ 1) for i in range(count)]
    far = [(i, i + 1) for i in range(1, count - 1, 2)]
    far += [(j, i) for i, j in far]
    return near, far


def body(fields, source_field, params_a, params_b, running_means, running_squares, running_cross):
    bricks = lax.axis_size("brick")
    near_route, far_route = routes(bricks)
    brick = lax.axis_index("brick")
    count = fields.shape[0]
    inside = (brick > 0) & (brick < bricks - 1)
    place = jnp.stack([lax.axis_index("side") * count, brick & 1, inside.astype(brick.dtype)])
    table = jnp.concatenate([params_a, params_b, place.astype(jnp.float32)])
    raw = fields[:, 0]
    source = source_field[0]
    send = lambda x, route: lax.ppermute(x, "brick", route)
    ny, nz = source.shape
    half = (count + 1) // 2
    halves = (raw[:half], raw[half:])
    flat_shape = (raw.size // 128, 128)
    far = send(raw, far_route)
    pairs = [x for piece in halves for x in (piece, send(piece, near_route))]
    beyond, partial, source = call(
        send_kernel, "send_planes", (table,), (source, *pairs), (flat_shape, raw.shape, source.shape), raw.size
    )
    beyond = send(beyond, far_route)
    ahead = call(
        first_kernel, "first_step", (table,), (partial, far), [piece.shape for piece in halves], raw.size
    )
    pairs = [x for piece in ahead for x in (piece, send(piece, near_route))]
    (far_part,) = call(far_kernel, "far_step", (table,), (far, *halves), (raw.shape,), raw.size)
    (mine,) = call(second_kernel, "second_step", (table,), (source, far_part, *pairs), (flat_shape,), raw.size)
    (mine,) = call(add_kernel, "add_beyond", (), (mine, beyond), (flat_shape,), raw.size // 8)
    strips = lax.all_to_all(
        mine.reshape(256, 1, count * 256), ("side", "brick"), split_axis=0, concat_axis=0, tiled=True
    )
    gathered = strips.reshape(2, 128 * 2 * count, 128)
    flat = lambda x: x.reshape(x.shape[0], 256, 128)
    outs = accumulate(
        gathered, count, flat(running_means), flat(running_squares), flat(running_cross)
    )
    return tuple(o.reshape(o.shape[0], 128, 1, 256) for o in outs)


def solution(mesh):
    strips = P(None, None, ("side", "brick"), None)
    return jax.shard_map(
        body,
        mesh=mesh,
        in_specs=(
            P("side", "brick", None, None),
            P("brick", None, None),
            P(),
            P(),
            strips,
            strips,
            strips,
        ),
        out_specs=(strips, strips, strips, strips),
        check_vma=False,
    )
```

```python
import functools

import jax
import jax.numpy as jnp
import numpy as np
from jax import lax
from jax.experimental import pallas as pl
from jax.experimental.pallas import tpu as pltpu
from jax.sharding import PartitionSpec as P

PRIOR = 3
LOWER = np.asarray((0.02, 0.02, 0.02, 0.01, 0.0, 0.0, 0.5, 0.0), np.float32)
UPPER = np.asarray((0.12, 0.12, 0.12, 0.06, 0.2, 1.0, 1.5, 0.1), np.float32)
WIDTH = UPPER - LOWER
ROWS = 64


def weights_of(table_ref, m):
    member = table_ref[16] + jnp.asarray(m, jnp.float32)
    values = []
    for k in range(8):
        from_b = (member == 1.0) | (member == float(k + 2))
        unit = jnp.where(from_b, table_ref[8 + k], table_ref[k])
        values.append(float(LOWER[k]) + float(WIDTH[k]) * unit)
    drift_1, drift_2, drift_3, diffusion, decay, amplitude, anisotropy, reaction = values
    along = diffusion * anisotropy
    before = drift_1 + diffusion
    near_w = jnp.where(table_ref[17] == 0.0, diffusion, before)
    far_w = jnp.where(table_ref[17] == 0.0, before, diffusion)
    own_w = 1.0 - drift_1 - drift_2 - drift_3 - decay - diffusion * (4.0 + 2.0 * anisotropy)
    return own_w, near_w, far_w, drift_2 + diffusion, diffusion, drift_3 + along, along, amplitude, reaction


def step_plane(shape, weights, load, near, rest, store):
    own_w, near_w, _, y_before_w, y_after_w, z_before_w, z_after_w, _, reaction = weights
    ny, nz = shape
    column = lax.broadcasted_iota(jnp.int32, (ROWS, nz), 1)
    zero = jnp.zeros((8, nz), jnp.float32)
    for r in range(0, ny, ROWS):
        c = load(r, ROWS)
        above = load(r - 8, 8) if r > 0 else zero
        below = load(r + ROWS, 8) if r + ROWS < ny else zero
        wide = jnp.concatenate([above, c, below], axis=0)
        y_before = pltpu.roll(wide, 1, 0)[8 : 8 + ROWS]
        y_after = pltpu.roll(wide, ROWS + 15, 0)[8 : 8 + ROWS]
        z_before = jnp.where(column == 0, 0.0, pltpu.roll(c, 1, 1))
        z_after = jnp.where(column == nz - 1, 0.0, pltpu.roll(c, nz - 1, 1))
        new = (
            c * (own_w - reaction * jnp.abs(c))
            + near_w * near(r, ROWS)
            + y_before_w * y_before
            + y_after_w * y_after
            + z_before_w * z_before
            + z_after_w * z_after
            + rest(r, ROWS)
        )
        store(r, new)


def reader(ref, *at):
    return lambda r, n: ref[(*at, slice(r, r + n), slice(None))]


def store_strips(out_ref, m, count, r, new):
    pieces = new.shape[1] // 128
    pitch = count * pieces
    for h in range(pieces):
        start = r * pitch + m * pieces + h
        out_ref[pl.ds(start, new.shape[0], stride=pitch), :] = new[:, h * 128 : (h + 1) * 128]


def send_kernel(table_ref, source_ref, *refs):
    pieces, (out_ref, partial_ref, source_copy_ref) = refs[:-3], refs[-3:]
    count, ny, nz = partial_ref.shape
    for r in range(0, ny, ROWS):
        source_copy_ref[r : r + ROWS, :] = source_ref[r : r + ROWS, :]
    first = 0
    for raw_ref, near_ref in zip(pieces[::2], pieces[1::2]):

        def one_member(j, carry, raw_ref=raw_ref, near_ref=near_ref, first=first):
            m = first + j
            weights = weights_of(table_ref, m)
            near_w, amplitude = weights[1], weights[7]
            for r in range(0, ny, ROWS):
                rows = slice(r, r + ROWS)
                rest = near_w * near_ref[j, rows, :] + amplitude * source_ref[rows, :]
                store_strips(out_ref, m, count, r, near_w * rest)

            def store(r, new):
                partial_ref[m, r : r + ROWS, :] = new

            rest = lambda r, n: amplitude * source_ref[r : r + n, :]
            step_plane((ny, nz), weights, reader(raw_ref, j), reader(near_ref, j), rest, store)
            return carry

        lax.fori_loop(0, raw_ref.shape[0], one_member, 0)
        first += raw_ref.shape[0]


def first_kernel(table_ref, partial_ref, far_ref, *out_refs):
    first = 0
    ny = far_ref.shape[1]
    for out_ref in out_refs:

        def one_member(j, carry, out_ref=out_ref, first=first):
            m = first + j
            far_w = weights_of(table_ref, m)[2]
            for r in range(0, ny, ROWS):
                rows = slice(r, r + ROWS)
                out_ref[j, rows, :] = partial_ref[m, rows, :] + far_w * far_ref[m, rows, :]
            return carry

        lax.fori_loop(0, out_ref.shape[0], one_member, 0)
        first += out_ref.shape[0]


def far_kernel(table_ref, raw_far_ref, *refs):
    pieces, out_ref = refs[:-1], refs[-1]
    inside = table_ref[18] > 0.0
    first = 0
    for raw_ref in pieces:

        def one_member(j, carry, raw_ref=raw_ref, first=first):
            m = first + j
            weights = weights_of(table_ref, m)
            far_w = weights[2]

            def store(r, new):
                out_ref[m, r : r + ROWS, :] = jnp.where(inside, far_w * new, 0.0)

            step_plane(
                out_ref.shape[1:], weights, reader(raw_far_ref, m), reader(raw_ref, j), lambda r, n: 0.0, store
            )
            return carry

        lax.fori_loop(0, raw_ref.shape[0], one_member, 0)
        first += raw_ref.shape[0]


def second_kernel(table_ref, source_ref, far_part_ref, *refs):
    out_ref = refs[-1]
    count, ny, nz = far_part_ref.shape
    first = 0
    for own_ref, near_ref in zip(refs[:-1:2], refs[1:-1:2]):

        def one_member(j, carry, own_ref=own_ref, near_ref=near_ref, first=first):
            m = first + j
            weights = weights_of(table_ref, m)
            amplitude = weights[7]
            rest = lambda r, n: far_part_ref[m, r : r + n, :] + amplitude * source_ref[r : r + n, :]
            step_plane(
                (ny, nz), weights, reader(own_ref, j), reader(near_ref, j), rest,
                lambda r, new: store_strips(out_ref, m, count, r, new),
            )
            return carry

        lax.fori_loop(0, own_ref.shape[0], one_member, 0)
        first += own_ref.shape[0]


def add_kernel(first_ref, second_ref, out_ref):
    rows = 320

    def some_rows(i, carry):
        at = pl.ds(pl.multiple_of(i * rows, rows), rows)
        out_ref[at, :] = first_ref[at, :] + second_ref[at, :]
        return carry

    lax.fori_loop(0, out_ref.shape[0] // rows, some_rows, 0)


def call(kernel, name, scalars, arrays, out_shapes, cells):
    whole = pl.BlockSpec(memory_space=pltpu.VMEM)
    return pl.pallas_call(
        kernel,
        in_specs=[pl.BlockSpec(memory_space=pltpu.SMEM)] * len(scalars) + [whole] * len(arrays),
        out_specs=[whole] * len(out_shapes),
        out_shape=[jax.ShapeDtypeStruct(shape, jnp.float32) for shape in out_shapes],
        compiler_params=pltpu.CompilerParams(vmem_limit_bytes=32 * 1024 * 1024),
        cost_estimate=pl.CostEstimate(flops=cells // 64, bytes_accessed=cells // 64, transcendentals=0),
        name=name,
    )(*scalars, *arrays)


def accumulate_kernel(count, blocks_of, gathered, means_ref, squares_ref, cross_ref, *refs):
    outs, blocks, (held, copied) = refs[:4], refs[4:8], refs[8:]
    new_means_ref, new_squares_ref, new_cross_ref, maps_ref = blocks
    copies = []
    start = 0
    for i, xb in enumerate(blocks_of):
        rows = pl.ds(2 * start, 2 * xb)
        for s in range(2):
            for m in range(count):
                for h in range(2):
                    held[s * count + m, pl.ds(h, xb, stride=2), :] = gathered[
                        s, pl.ds(start * 2 * count + m * 2 + h, xb, stride=2 * count), :
                    ]

        def moments(m):
            out, mean = held[m, : 2 * xb, :], means_ref[m, rows, :]
            deviation = out - mean
            new_mean = mean + deviation * (1.0 / (PRIOR + 1))
            after = out - new_mean
            new_square = squares_ref[m, rows, :] + deviation * after
            new_means_ref[m, rows, :] = new_mean
            new_squares_ref[m, rows, :] = new_square
            return deviation, after, new_square

        base = [moments(0), moments(1)]
        for m in range(2, 2 * count):
            k = m - 2
            _, after, new_square = moments(m)
            first_cross = cross_ref[k, rows, :] + base[1][0] * after
            total_cross = cross_ref[8 + k, rows, :] + base[0][0] * after
            new_cross_ref[k, rows, :] = first_cross
            new_cross_ref[8 + k, rows, :] = total_cross
            maps_ref[k, rows, :] = first_cross * lax.rsqrt(base[1][2] * new_square)
            maps_ref[8 + k, rows, :] = 1.0 - total_cross * lax.rsqrt(base[0][2] * new_square)
        for j, (block, out) in enumerate(zip(blocks, outs)):
            copy = pltpu.make_async_copy(block.at[:, rows], out.at[:, rows], copied.at[i, j])
            copy.start()
            copies.append(copy)
        start += xb
    for copy in copies:
        copy.wait()


def accumulate(gathered, count, means, squares, cross):
    blocks_of = (8, 16, 40, 64)
    nx = sum(blocks_of)
    whole = pl.BlockSpec(memory_space=pltpu.VMEM)
    shape = lambda lead: (lead, 2 * nx, 128)
    leads = (10, 10, 16, 16)
    return pl.pallas_call(
        functools.partial(accumulate_kernel, count, blocks_of),
        in_specs=[whole] * 4,
        out_specs=[pl.BlockSpec(memory_space=pl.ANY)] * 4,
        out_shape=[jax.ShapeDtypeStruct(shape(lead), jnp.float32) for lead in leads],
        scratch_shapes=[pltpu.VMEM(shape(lead), jnp.float32) for lead in leads]
        + [pltpu.VMEM((10, 2 * max(blocks_of), 128), jnp.float32), pltpu.SemaphoreType.DMA((len(blocks_of), 4))],
        compiler_params=pltpu.CompilerParams(vmem_limit_bytes=32 * 1024 * 1024),
        cost_estimate=pl.CostEstimate(
            flops=40 * 10 * nx * 256, bytes_accessed=13 * 1024 * 1024, transcendentals=16 * nx * 256
        ),
        name="accumulate",
    )(gathered, means, squares, cross)


def routes(count):
    near = [(i, i ^ 1) for i in range(count)]
    far = [(i, i + 1) for i in range(1, count - 1, 2)]
    far += [(j, i) for i, j in far]
    return near, far


def body(fields, source_field, params_a, params_b, running_means, running_squares, running_cross):
    bricks = lax.axis_size("brick")
    near_route, far_route = routes(bricks)
    brick = lax.axis_index("brick")
    count = fields.shape[0]
    inside = (brick > 0) & (brick < bricks - 1)
    place = jnp.stack([lax.axis_index("side") * count, brick & 1, inside.astype(brick.dtype)])
    table = jnp.concatenate([params_a, params_b, place.astype(jnp.float32)])
    raw = fields[:, 0]
    source = source_field[0]
    send = lambda x, route: lax.ppermute(x, "brick", route)
    ny, nz = source.shape
    half = (count + 1) // 2
    halves = (raw[:half], raw[half:])
    flat_shape = (raw.size // 128, 128)
    far = send(raw, far_route)
    pairs = [x for piece in halves for x in (piece, send(piece, near_route))]
    beyond, partial, source = call(
        send_kernel, "send_planes", (table,), (source, *pairs), (flat_shape, raw.shape, source.shape), raw.size
    )
    beyond = send(beyond, far_route)
    ahead = call(
        first_kernel, "first_step", (table,), (partial, far), [piece.shape for piece in halves], raw.size
    )
    pairs = [x for piece in ahead for x in (piece, send(piece, near_route))]
    (far_part,) = call(far_kernel, "far_step", (table,), (far, *halves), (raw.shape,), raw.size)
    (mine,) = call(second_kernel, "second_step", (table,), (source, far_part, *pairs), (flat_shape,), raw.size)
    (mine,) = call(add_kernel, "add_beyond", (), (mine, beyond), (flat_shape,), raw.size // 8)
    strips = lax.all_to_all(
        mine.reshape(256, 1, count * 256), ("side", "brick"), split_axis=0, concat_axis=0, tiled=True
    )
    gathered = strips.reshape(2, 128 * 2 * count, 128)
    flat = lambda x: x.reshape(x.shape[0], 256, 128)
    outs = accumulate(
        gathered, count, flat(running_means), flat(running_squares), flat(running_cross)
    )
    return tuple(o.reshape(o.shape[0], 128, 1, 256) for o in outs)


def solution(mesh):
    strips = P(None, None, ("side", "brick"), None)
    return jax.shard_map(
        body,
        mesh=mesh,
        in_specs=(
            P("side", "brick", None, None),
            P("brick", None, None),
            P(),
            P(),
            strips,
            strips,
            strips,
        ),
        out_specs=(strips, strips, strips, strips),
        check_vma=False,
    )
```

```python
import functools

import jax
import jax.numpy as jnp
import numpy as np
from jax import lax
from jax.experimental import pallas as pl
from jax.experimental.pallas import tpu as pltpu
from jax.sharding import PartitionSpec as P

PRIOR = 3
LOWER = np.asarray((0.02, 0.02, 0.02, 0.01, 0.0, 0.0, 0.5, 0.0), np.float32)
UPPER = np.asarray((0.12, 0.12, 0.12, 0.06, 0.2, 1.0, 1.5, 0.1), np.float32)
WIDTH = UPPER - LOWER
ROWS = 64


def weights_of(table_ref, m):
    member = table_ref[16] + jnp.asarray(m, jnp.float32)
    values = []
    for k in range(8):
        from_b = (member == 1.0) | (member == float(k + 2))
        unit = jnp.where(from_b, table_ref[8 + k], table_ref[k])
        values.append(float(LOWER[k]) + float(WIDTH[k]) * unit)
    drift_1, drift_2, drift_3, diffusion, decay, amplitude, anisotropy, reaction = values
    along = diffusion * anisotropy
    before = drift_1 + diffusion
    near_w = jnp.where(table_ref[17] == 0.0, diffusion, before)
    far_w = jnp.where(table_ref[17] == 0.0, before, diffusion)
    own_w = 1.0 - drift_1 - drift_2 - drift_3 - decay - diffusion * (4.0 + 2.0 * anisotropy)
    return own_w, near_w, far_w, drift_2 + diffusion, diffusion, drift_3 + along, along, amplitude, reaction


def step_plane(shape, weights, load, near, rest, store):
    own_w, near_w, _, y_before_w, y_after_w, z_before_w, z_after_w, _, reaction = weights
    ny, nz = shape
    column = lax.broadcasted_iota(jnp.int32, (ROWS, nz), 1)
    zero = jnp.zeros((8, nz), jnp.float32)
    for r in range(0, ny, ROWS):
        c = load(r, ROWS)
        above = load(r - 8, 8) if r > 0 else zero
        below = load(r + ROWS, 8) if r + ROWS < ny else zero
        wide = jnp.concatenate([above, c, below], axis=0)
        y_before = pltpu.roll(wide, 1, 0)[8 : 8 + ROWS]
        y_after = pltpu.roll(wide, ROWS + 15, 0)[8 : 8 + ROWS]
        z_before = jnp.where(column == 0, 0.0, pltpu.roll(c, 1, 1))
        z_after = jnp.where(column == nz - 1, 0.0, pltpu.roll(c, nz - 1, 1))
        new = (
            c * (own_w - reaction * jnp.abs(c))
            + near_w * near(r, ROWS)
            + y_before_w * y_before
            + y_after_w * y_after
            + z_before_w * z_before
            + z_after_w * z_after
            + rest(r, ROWS)
        )
        store(r, new)


def reader(ref, *at):
    return lambda r, n: ref[(*at, slice(r, r + n), slice(None))]


def store_strips(out_ref, m, count, r, new):
    pieces = new.shape[1] // 128
    pitch = count * pieces
    for h in range(pieces):
        start = r * pitch + m * pieces + h
        out_ref[pl.ds(start, new.shape[0], stride=pitch), :] = new[:, h * 128 : (h + 1) * 128]


def send_kernel(table_ref, source_ref, *refs):
    pieces, (out_ref, partial_ref, source_copy_ref) = refs[:-3], refs[-3:]
    count, ny, nz = partial_ref.shape
    for r in range(0, ny, ROWS):
        source_copy_ref[r : r + ROWS, :] = source_ref[r : r + ROWS, :]
    first = 0
    for raw_ref, near_ref in zip(pieces[::2], pieces[1::2]):

        def one_member(j, carry, raw_ref=raw_ref, near_ref=near_ref, first=first):
            m = first + j
            weights = weights_of(table_ref, m)
            near_w, amplitude = weights[1], weights[7]
            for r in range(0, ny, ROWS):
                rows = slice(r, r + ROWS)
                rest = near_w * near_ref[j, rows, :] + amplitude * source_ref[rows, :]
                store_strips(out_ref, m, count, r, near_w * rest)

            def store(r, new):
                partial_ref[m, r : r + ROWS, :] = new

            rest = lambda r, n: amplitude * source_ref[r : r + n, :]
            step_plane((ny, nz), weights, reader(raw_ref, j), reader(near_ref, j), rest, store)
            return carry

        lax.fori_loop(0, raw_ref.shape[0], one_member, 0)
        first += raw_ref.shape[0]


def first_kernel(table_ref, partial_ref, far_ref, *out_refs):
    first = 0
    ny = far_ref.shape[1]
    for out_ref in out_refs:

        def one_member(j, carry, out_ref=out_ref, first=first):
            m = first + j
            far_w = weights_of(table_ref, m)[2]
            for r in range(0, ny, ROWS):
                rows = slice(r, r + ROWS)
                out_ref[j, rows, :] = partial_ref[m, rows, :] + far_w * far_ref[m, rows, :]
            return carry

        lax.fori_loop(0, out_ref.shape[0], one_member, 0)
        first += out_ref.shape[0]


def far_kernel(table_ref, raw_far_ref, *refs):
    pieces, out_ref = refs[:-1], refs[-1]
    inside = table_ref[18] > 0.0
    first = 0
    for raw_ref in pieces:

        def one_member(j, carry, raw_ref=raw_ref, first=first):
            m = first + j
            weights = weights_of(table_ref, m)
            far_w = weights[2]

            def store(r, new):
                out_ref[m, r : r + ROWS, :] = jnp.where(inside, far_w * new, 0.0)

            step_plane(
                out_ref.shape[1:], weights, reader(raw_far_ref, m), reader(raw_ref, j), lambda r, n: 0.0, store
            )
            return carry

        lax.fori_loop(0, raw_ref.shape[0], one_member, 0)
        first += raw_ref.shape[0]


def second_kernel(table_ref, source_ref, far_part_ref, *refs):
    out_ref = refs[-1]
    count, ny, nz = far_part_ref.shape
    first = 0
    for own_ref, near_ref in zip(refs[:-1:2], refs[1:-1:2]):

        def one_member(j, carry, own_ref=own_ref, near_ref=near_ref, first=first):
            m = first + j
            weights = weights_of(table_ref, m)
            amplitude = weights[7]
            rest = lambda r, n: far_part_ref[m, r : r + n, :] + amplitude * source_ref[r : r + n, :]
            step_plane(
                (ny, nz), weights, reader(own_ref, j), reader(near_ref, j), rest,
                lambda r, new: store_strips(out_ref, m, count, r, new),
            )
            return carry

        lax.fori_loop(0, own_ref.shape[0], one_member, 0)
        first += own_ref.shape[0]


def add_kernel(first_ref, second_ref, out_ref):
    rows = 320

    def some_rows(i, carry):
        at = pl.ds(pl.multiple_of(i * rows, rows), rows)
        out_ref[at, :] = first_ref[at, :] + second_ref[at, :]
        return carry

    lax.fori_loop(0, out_ref.shape[0] // rows, some_rows, 0)


def call(kernel, name, scalars, arrays, out_shapes, cells):
    whole = pl.BlockSpec(memory_space=pltpu.VMEM)
    return pl.pallas_call(
        kernel,
        in_specs=[pl.BlockSpec(memory_space=pltpu.SMEM)] * len(scalars) + [whole] * len(arrays),
        out_specs=[whole] * len(out_shapes),
        out_shape=[jax.ShapeDtypeStruct(shape, jnp.float32) for shape in out_shapes],
        compiler_params=pltpu.CompilerParams(vmem_limit_bytes=32 * 1024 * 1024),
        cost_estimate=pl.CostEstimate(flops=cells // 64, bytes_accessed=cells // 64, transcendentals=0),
        name=name,
    )(*scalars, *arrays)


def accumulate_kernel(count, blocks_of, gathered, means_ref, squares_ref, cross_ref, *refs):
    outs, blocks, (held, copied) = refs[:4], refs[4:8], refs[8:]
    new_means_ref, new_squares_ref, new_cross_ref, maps_ref = blocks
    copies = []
    start = 0
    for i, xb in enumerate(blocks_of):
        rows = pl.ds(2 * start, 2 * xb)
        for s in range(2):
            for m in range(count):
                for h in range(2):
                    held[s * count + m, pl.ds(h, xb, stride=2), :] = gathered[
                        s, pl.ds(start * 2 * count + m * 2 + h, xb, stride=2 * count), :
                    ]

        def moments(m):
            out, mean = held[m, : 2 * xb, :], means_ref[m, rows, :]
            deviation = out - mean
            new_mean = mean + deviation * (1.0 / (PRIOR + 1))
            after = out - new_mean
            new_square = squares_ref[m, rows, :] + deviation * after
            new_means_ref[m, rows, :] = new_mean
            new_squares_ref[m, rows, :] = new_square
            return deviation, after, new_square

        base = [moments(0), moments(1)]
        for m in range(2, 2 * count):
            k = m - 2
            _, after, new_square = moments(m)
            first_cross = cross_ref[k, rows, :] + base[1][0] * after
            total_cross = cross_ref[8 + k, rows, :] + base[0][0] * after
            new_cross_ref[k, rows, :] = first_cross
            new_cross_ref[8 + k, rows, :] = total_cross
            maps_ref[k, rows, :] = first_cross * lax.rsqrt(base[1][2] * new_square)
            maps_ref[8 + k, rows, :] = 1.0 - total_cross * lax.rsqrt(base[0][2] * new_square)
        for j, (block, out) in enumerate(zip(blocks, outs)):
            copy = pltpu.make_async_copy(block.at[:, rows], out.at[:, rows], copied.at[i, j])
            copy.start()
            copies.append(copy)
        start += xb
    for copy in copies:
        copy.wait()


def accumulate(gathered, count, means, squares, cross):
    blocks_of = (8, 12, 20, 32, 56)
    nx = sum(blocks_of)
    whole = pl.BlockSpec(memory_space=pltpu.VMEM)
    shape = lambda lead: (lead, 2 * nx, 128)
    leads = (10, 10, 16, 16)
    return pl.pallas_call(
        functools.partial(accumulate_kernel, count, blocks_of),
        in_specs=[whole] * 4,
        out_specs=[pl.BlockSpec(memory_space=pl.ANY)] * 4,
        out_shape=[jax.ShapeDtypeStruct(shape(lead), jnp.float32) for lead in leads],
        scratch_shapes=[pltpu.VMEM(shape(lead), jnp.float32) for lead in leads]
        + [pltpu.VMEM((10, 2 * max(blocks_of), 128), jnp.float32), pltpu.SemaphoreType.DMA((len(blocks_of), 4))],
        compiler_params=pltpu.CompilerParams(vmem_limit_bytes=32 * 1024 * 1024),
        cost_estimate=pl.CostEstimate(
            flops=40 * 10 * nx * 256, bytes_accessed=13 * 1024 * 1024, transcendentals=16 * nx * 256
        ),
        name="accumulate",
    )(gathered, means, squares, cross)


def routes(count):
    near = [(i, i ^ 1) for i in range(count)]
    far = [(i, i + 1) for i in range(1, count - 1, 2)]
    far += [(j, i) for i, j in far]
    return near, far


def body(fields, source_field, params_a, params_b, running_means, running_squares, running_cross):
    bricks = lax.axis_size("brick")
    near_route, far_route = routes(bricks)
    brick = lax.axis_index("brick")
    count = fields.shape[0]
    inside = (brick > 0) & (brick < bricks - 1)
    place = jnp.stack([lax.axis_index("side") * count, brick & 1, inside.astype(brick.dtype)])
    table = jnp.concatenate([params_a, params_b, place.astype(jnp.float32)])
    raw = fields[:, 0]
    source = source_field[0]
    send = lambda x, route: lax.ppermute(x, "brick", route)
    ny, nz = source.shape
    half = (count + 1) // 2
    halves = (raw[:half], raw[half:])
    flat_shape = (raw.size // 128, 128)
    far = send(raw, far_route)
    pairs = [x for piece in halves for x in (piece, send(piece, near_route))]
    beyond, partial, source = call(
        send_kernel, "send_planes", (table,), (source, *pairs), (flat_shape, raw.shape, source.shape), raw.size
    )
    beyond = send(beyond, far_route)
    ahead = call(
        first_kernel, "first_step", (table,), (partial, far), [piece.shape for piece in halves], raw.size
    )
    pairs = [x for piece in ahead for x in (piece, send(piece, near_route))]
    (far_part,) = call(far_kernel, "far_step", (table,), (far, *halves), (raw.shape,), raw.size)
    (mine,) = call(second_kernel, "second_step", (table,), (source, far_part, *pairs), (flat_shape,), raw.size)
    (mine,) = call(add_kernel, "add_beyond", (), (mine, beyond), (flat_shape,), raw.size // 8)
    strips = lax.all_to_all(
        mine.reshape(256, 1, count * 256), ("side", "brick"), split_axis=0, concat_axis=0, tiled=True
    )
    gathered = strips.reshape(2, 128 * 2 * count, 128)
    flat = lambda x: x.reshape(x.shape[0], 256, 128)
    outs = accumulate(
        gathered, count, flat(running_means), flat(running_squares), flat(running_cross)
    )
    return tuple(o.reshape(o.shape[0], 128, 1, 256) for o in outs)


def solution(mesh):
    strips = P(None, None, ("side", "brick"), None)
    return jax.shard_map(
        body,
        mesh=mesh,
        in_specs=(
            P("side", "brick", None, None),
            P("brick", None, None),
            P(),
            P(),
            strips,
            strips,
            strips,
        ),
        out_specs=(strips, strips, strips, strips),
        check_vma=False,
    )
```
